32 devices in a mesh: member: 4 (over x, core), shard: 8 (over z, y).
Axes of the slice: x: 2, y: 2, z: 4, core: 2. Of those that a mesh axis runs over, the one named last changes fastest.
Arguments:
- latent: bfloat16 [4, 256, 1024], P('member', 'shard'), may hold values from -6 to 6
- grid_embed: bfloat16 [2048, 1024], P('shard'), may hold values from -6 to 6
- edge_src: int32 [2048, 3], P('shard'), may hold values from 0 to 255, as said below
- area: float32 [2048], P('shard'), may hold values from 0.15 to 27
- target: float32 [2048, 100], P('shard'), may hold values from -6 to 6
- w_query: bfloat16 [1024, 1024], replicated, may hold values from -0.1875 to 0.1875
- w_keyval: bfloat16 [1024, 2048], replicated, may hold values from -0.1875 to 0.1875
- w_head: bfloat16 [1024, 100], replicated, may hold values from -0.1875 to 0.1875
Outputs:
- loss: float32 [4], P('member')
- d_latent: float32 [4, 256, 1024], P('member', 'shard')
- grad_query: float32 [1024, 1024], P('shard')
- grad_keyval: float32 [1024, 2048], P('shard')
- grad_head: float32 [1024, 100], P('shard')
The draws below stay inside these ranges and needn't reach their ends.
Inputs may be any that keep to these rules, and one draw needn't show every extreme that they name: edge_src[g, k] is a node of the latent block of index g // 256 or of one of the two blocks beside it, cyclically, where block b holds nodes b * 32 to (b + 1) * 32 - 1.
All inputs are finite; a program needn't handle non-finite values.
Results may differ from the reference program's by a relative error of at most 0.035.
Values may be sent and summed in bfloat16 or wider, within the bound.
A program may use at most 128 MiB of HBM per device.

```python
import math
import jax
import jax.numpy as jnp
from jax import lax

D = 1024
HEADS = 16
VARS = 100
KNB = 3
G_DEV = 256
H_DEV = 32
GN = 2048
HN = 256
MEMBERS = 4
N_SHARD = 8


def draw_edge_src(key, part):
    key = jax.random.fold_in(key, 11)
    first, second = jax.random.split(key)
    owner = jnp.arange(GN, dtype=jnp.int32) // G_DEV
    offsets = jax.random.randint(first, (GN, KNB), -1, 2, dtype=jnp.int32)
    within = jax.random.randint(second, (GN, KNB), 0, H_DEV, dtype=jnp.int32)
    block = jnp.mod(owner[:, None] + offsets, N_SHARD)
    return (block * H_DEV + within).astype(jnp.int32)


def draw_area(key, part):
    key = jax.random.fold_in(key, 23)
    points = jnp.arange(GN, dtype=jnp.int32)
    across = (points // G_DEV).astype(jnp.float32) / (N_SHARD - 1)
    inside = (points % G_DEV).astype(jnp.float32) / G_DEV
    ramp = (1.0 + 2.0 * across) * (1.0 + 2.0 * inside)
    base = jnp.exp(jax.random.uniform(key, (GN,), jnp.float32, jnp.log(0.3), jnp.log(3.0)))
    return (base * ramp).astype(jnp.float32)


def raised(entries, rng, source, target, shards_of, factor):
    def block_of(dim):
        return (jnp.arange(entries.shape[dim]) // (entries.shape[dim] // shards_of)).reshape((-1,) + (1,) * (entries.ndim - 1 - dim))

    near = jax.random.permutation(rng, shards_of)[block_of(target)]
    far = (block_of(target) + shards_of // 2) % shards_of
    return jnp.where((block_of(source) == near) | (block_of(source) == far), factor * entries, entries)


def level_of(stream_key, extent, pieces, low, high):
    def one(dim, parts):
        steps = jax.random.uniform(jax.random.fold_in(jax.random.fold_in(stream_key, 6), dim), (parts,), jnp.float32, low / len(pieces), high / len(pieces))
        return jnp.repeat(jnp.exp(steps), extent[dim] // parts).reshape((-1,) + (1,) * (len(extent) - dim - 1))

    factor_of = one(*pieces[0])
    for cut in pieces[1:]:
        factor_of = factor_of * one(*cut)
    return factor_of


def noise(stream_key, shape, scale, reach, cuts=(), kind=jnp.bfloat16):
    gain = level_of(stream_key, shape, cuts, -0.22, 0.18) if cuts else 1.0
    drawn = jax.random.normal(stream_key, shape, jnp.float32) * scale * gain
    return jnp.minimum(jnp.maximum(drawn, -reach), reach).astype(kind)


def heavy_noise(stream_key, dims, deviation, reach, shards, heavy, kind=jnp.bfloat16):
    values = deviation * jax.random.normal(stream_key, dims, jnp.float32)
    if shards:
        values = values * level_of(stream_key, dims, shards, -0.22, 0.18)
    return jnp.clip(raised(values, jax.random.fold_in(stream_key, 3), *heavy), -reach, reach).astype(kind)


def setup_inputs(seed: int = 0) -> dict:
    streams_of = jax.random.split(jax.random.key(seed), 9)
    return {
        "latent": heavy_noise(streams_of[0], (MEMBERS, HN, D), 1.0, 6.0, ((0, 4), (1, 8)), (1, 2, 8, 2.0)),
        "grid_embed": heavy_noise(streams_of[1], (GN, D), 1.0, 6.0, ((0, 8),), (0, 1, 8, 2.0)),
        "edge_src": draw_edge_src(jax.random.fold_in(streams_of[8], 71), 0),
        "area": draw_area(jax.random.fold_in(streams_of[8], 71), 0),
        "target": noise(streams_of[4], (GN, VARS), 1.0, 6.0, ((0, 8),), jnp.float32),
        "w_query": noise(streams_of[5], (D, D), D ** -0.5, 0.1875),
        "w_keyval": noise(streams_of[6], (D, 2 * D), D ** -0.5, 0.1875),
        "w_head": noise(streams_of[7], (D, VARS), D ** -0.5, 0.1875),
    }


def normalize_heads(values):
    shaped = values.reshape(values.shape[:-1] + (HEADS, values.shape[-1] // HEADS))
    return shaped * lax.rsqrt(lax.optimization_barrier(jnp.mean(shaped * shaped, -1, keepdims=True)) + 1e-06)

def attend(query, table, source):
    width = query.shape[-1]
    size = width // HEADS
    picked = table[source]
    query_norm = normalize_heads(query)
    key_norm = normalize_heads(picked[..., :width])
    values = picked[..., width:].reshape(picked.shape[:2] + (HEADS, size))
    score = jnp.einsum('bhs,bkhs->bhk', query_norm, key_norm) * size ** (-0.5)
    expon = jnp.exp(score)
    weight = expon / lax.optimization_barrier(jnp.sum(expon, -1, keepdims=True))
    return jnp.einsum('bhk,bkhs->bhs', weight, values).reshape(query.shape)

def layer_norm(hidden):
    center = hidden - lax.optimization_barrier(jnp.mean(hidden, -1, keepdims=True))
    return center * lax.rsqrt(lax.optimization_barrier(jnp.mean(center * center, -1, keepdims=True)) + 1e-05)

def smooth_abs(delta):
    return jnp.sqrt(delta * delta + 0.0625)

def slope(delta):
    return delta / smooth_abs(delta)

def reference(latent, grid_embed, edge_src, area, target, w_query, w_keyval, w_head):
    members = latent.shape[0]
    rows = grid_embed.shape[0]
    width = grid_embed.shape[1]
    block = math.gcd(rows, 512)
    blocks = rows // block
    query = jnp.dot(grid_embed, w_query, preferred_element_type=jnp.float32)
    query_blocks = query.reshape(blocks, block, width)
    source_blocks = edge_src.reshape(blocks, block, KNB)
    embed_wide = grid_embed.astype(jnp.float32)

    def make_table(member_latent):
        rounded = jnp.dot(member_latent, w_keyval, preferred_element_type=jnp.float32).astype(jnp.bfloat16)
        return lax.optimization_barrier(rounded).astype(jnp.float32)

    def forward_hidden(table):
        mixed = lax.map(lambda pair: attend(pair[0], table, pair[1]), (query_blocks, source_blocks))
        return embed_wide + mixed.reshape(rows, width)

    def forward(member_latent):
        hidden = forward_hidden(make_table(member_latent))
        normed = layer_norm(hidden).astype(jnp.bfloat16)
        return jnp.dot(normed, w_head, preferred_element_type=jnp.float32)
    preds = lax.map(forward, latent)
    miss = preds - target[None]
    pair_value = jnp.zeros_like(preds)
    pair_slope = jnp.zeros_like(preds)
    for other in range(members):
        delta = preds - preds[other][None]
        pair_value = pair_value + smooth_abs(delta)
        pair_slope = pair_slope + slope(delta)
    pair_value = pair_value - 0.25
    weights = area[None, :, None]
    crps_terms = smooth_abs(miss) / members - pair_value / (2.0 * members * (members - 1))
    loss = lax.optimization_barrier(jnp.sum(weights * crps_terms, axis=(1, 2))) / (rows * target.shape[1])
    d_pred = weights * (slope(miss) / members - pair_slope / (members * (members - 1)))

    def backward(pair):
        member_latent, d_out = pair
        table = make_table(member_latent)
        hidden = forward_hidden(table)
        normed = layer_norm(hidden).astype(jnp.bfloat16)
        d_outb = d_out.astype(jnp.bfloat16)
        grad_h = jnp.dot(normed.T, d_outb, preferred_element_type=jnp.float32)
        d_normed = jnp.dot(d_outb, w_head.T, preferred_element_type=jnp.float32)
        ignored, norm_back = jax.vjp(layer_norm, hidden)
        d_hidden = norm_back(d_normed)[0]

        def block_back(carry, items):
            query_part, source_part, d_part = items
            ignored_out, attend_back = jax.vjp(lambda qq, tt: attend(qq, tt, source_part), query_part, table)
            d_q, d_t = attend_back(d_part)
            return (carry + d_t, d_q)
        d_table, d_query = lax.scan(block_back, jnp.zeros(table.shape, jnp.float32), (query_blocks, source_blocks, d_hidden.reshape(blocks, block, width)))
        d_queryb = d_query.reshape(rows, width).astype(jnp.bfloat16)
        d_tableb = d_table.astype(jnp.bfloat16)
        grad_q = jnp.dot(grid_embed.T, d_queryb, preferred_element_type=jnp.float32)
        grad_kv = jnp.dot(member_latent.T, d_tableb, preferred_element_type=jnp.float32)
        d_lat = jnp.dot(d_tableb, w_keyval.T, preferred_element_type=jnp.float32)
        return (grad_q, grad_kv, grad_h, d_lat)
    grad_q, grad_kv, grad_h, d_latent = lax.map(backward, (latent, d_pred))
    scale = (members * rows) ** (-0.5)
    return (loss, d_latent, lax.optimization_barrier(jnp.sum(grad_q, 0)) * scale, lax.optimization_barrier(jnp.sum(grad_kv, 0)) * scale, lax.optimization_barrier(jnp.sum(grad_h, 0)) * scale)
```

```python
import functools

import jax
import jax.numpy as jnp
from jax import lax
from jax.experimental import pallas as pl
from jax.experimental.pallas import tpu as pltpu
from jax.sharding import PartitionSpec as P

HEADS = 16
LANES = 128
BF = jnp.bfloat16
F32 = jnp.float32
MESH = pl.DeviceIdType.MESH


def mm(a, b):
    return jnp.dot(a, b, preferred_element_type=F32)


def mm_nt(a, b):
    return lax.dot_general(a, b, (((1,), (1,)), ((), ())), preferred_element_type=F32)


def mm_tn(a, b):
    return lax.dot_general(a, b, (((0,), (0,)), ((), ())), preferred_element_type=F32)


def kernel(
    members, shards,
    latent, embed, source, area, target, w_query, w_keyval, w_head,
    loss_out, d_latent, grad_query, grad_keyval, grad_head,
    lat3, lat4, table, query, q_norm, q_rstd, k_norm, k_rstd, expo, recip, mixed, hidden, d_hid,
    wh, preds, preds_in, ph, ph_in, ph_fin, part, part_in,
    own_dt, halo, halo_in, ob, dt4, dqs, dqs_in, pq, yq, zq, zq_in, pk, yk, zk, zk_in, fq, fk, fq_in, fk_in,
    halo_sem, lat_sem, pred_sem, head_sem, loss_sem, hfin_sem, dth_sem, dtm_sem, dq_sem,
    y_sem, zq_sem, zk_sem, fq_sem, fk_sem,
):
    rows, width = embed.shape
    nodes = latent.shape[0]
    variables = target.shape[1]
    m = lax.axis_index("member")
    s = lax.axis_index("shard")
    size = width // HEADS
    pairs = width // LANES
    chunk = width // members
    per_chunk = chunk // LANES
    out_rows = width // shards
    outer = shards // 2
    a = s // 2
    b = lax.rem(s, 2)
    padded = lat3.shape[0]
    scale = (members * rows * shards) ** (-0.5)

    def send(src, dst, sems, index, to_m, to_s):
        return pltpu.make_async_remote_copy(
            src_ref=src, dst_ref=dst, send_sem=sems.at[0, index], recv_sem=sems.at[1, index],
            device_id=(to_m, to_s), device_id_type=MESH,
        )

    def member(i):
        return lax.rem(m + i, members)

    def shard(i):
        return lax.rem(s + i, shards)

    barrier = pltpu.get_barrier_semaphore()
    for i in range(1, members):
        pl.semaphore_signal(barrier, inc=1, device_id=(member(i), s), device_id_type=MESH)
    for i in range(1, shards):
        pl.semaphore_signal(barrier, inc=1, device_id=(m, shard(i)), device_id_type=MESH)
    pl.semaphore_wait(barrier, members + shards - 2)

    halo_up = send(latent, lat3.at[pl.ds(0, nodes)], halo_sem, 0, m, shard(1))
    halo_down = send(latent, lat3.at[pl.ds(2 * nodes, nodes)], halo_sem, 1, m, shard(shards - 1))
    halo_up.start()
    halo_down.start()
    lat_copies = [
        send(latent, lat4.at[pl.ds(i * nodes, nodes)], lat_sem, i, member(i), s) for i in range(1, members)
    ]
    for copy in lat_copies:
        copy.start()
    lat3[nodes : 2 * nodes, :] = latent[...]
    lat3[3 * nodes :, :] = jnp.zeros((padded - 3 * nodes, width), BF)
    lat4[:nodes, :] = latent[...]

    wh[...] = jnp.zeros(wh.shape, BF)
    wh[:, :variables] = w_head[...]

    def query_step(i, carry):
        cols = pl.ds(pl.multiple_of(i * 256, 256), 256)
        query[:, cols] = mm(embed[...], w_query[:, cols])
        return carry

    lax.fori_loop(0, width // 256, query_step, 0)

    lane = lax.broadcasted_iota(jnp.int32, (1, LANES), 1)
    masks = [(lane // size == h).astype(F32) for h in range(2)]
    row_head = lax.broadcasted_iota(jnp.int32, (LANES, LANES), 0) // size
    col_head = lax.broadcasted_iota(jnp.int32, (LANES, LANES), 1) // size
    same = jnp.where(row_head == col_head, 1.0 / size, 0.0).astype(BF)

    def head_mean(x):
        return mm(x.astype(BF), same)

    def stacked(x):
        return jnp.concatenate([x * masks[0], x * masks[1]], axis=0).astype(BF)

    def unstacked(x):
        return x[:padded] * masks[0] + x[padded:] * masks[1]

    ones = jnp.ones((padded, LANES), F32)
    in_head = stacked(ones)
    src = source[...] - (s - 1) * nodes
    src = jnp.where(src < 0, src + shards * nodes, src)
    src = jnp.where(src >= shards * nodes, src - shards * nodes, src)
    node = lax.broadcasted_iota(jnp.int32, (rows, padded), 1)
    count = jnp.zeros((rows, padded), F32)
    for k in range(source.shape[1]):
        count = count + (src[:, k : k + 1] == node).astype(F32)
    count2 = jnp.concatenate([count, count], axis=1)

    halo_up.wait()
    halo_down.wait()

    def table_step(i, carry):
        cols = pl.ds(pl.multiple_of(i * 256, 256), 256)
        table[:, cols] = mm(lat3[...], w_keyval[:, cols]).astype(BF)
        return carry

    lax.fori_loop(0, 2 * width // 256, table_step, 0)

    for p in range(pairs):
        cols = slice(p * LANES, (p + 1) * LANES)
        q = query[:, cols]
        r = lax.rsqrt(head_mean(q * q) + 1e-06)
        qn = (q * r).astype(BF)
        q_norm[:, cols] = qn
        q_rstd[:, cols] = r
        key = table[:, cols].astype(F32)
        rk = lax.rsqrt(head_mean(key * key) + 1e-06)
        kn = key * rk
        k_norm[:, cols] = kn
        k_rstd[:, cols] = rk
        score = mm_nt(qn, stacked(kn))
        e = (count2 * jnp.exp(score * size ** (-0.5))).astype(BF)
        expo[p] = e
        v2 = stacked(table[:, width + p * LANES : width + (p + 1) * LANES].astype(F32))
        both = mm(e, jnp.concatenate([v2, in_head], axis=1))
        inv = 1.0 / both[:, LANES:]
        out = both[:, :LANES] * inv
        recip[:, cols] = inv
        mixed[:, cols] = out
        hidden[:, cols] = embed[:, cols].astype(F32) + out

    hid = hidden[...]
    center = hid - jnp.mean(hid, -1, keepdims=True)
    rstd = lax.rsqrt(jnp.mean(center * center, -1, keepdims=True) + 1e-05)
    nhat = center * rstd
    hidden[...] = nhat
    normed = nhat.astype(BF)
    pred = mm(normed, wh[...])
    preds[...] = pred.astype(BF)
    pred_copies = [send(preds, preds_in.at[i], pred_sem, i, member(i), s) for i in range(1, members)]
    for copy in pred_copies:
        copy.start()
    valid = (lane < variables).astype(F32)
    weights = area[...]
    want = jnp.concatenate([target[...], jnp.zeros((rows, LANES - variables), F32)], axis=1)
    miss = pred - want
    miss_sq = miss * miss + 0.0625
    miss_inv = lax.rsqrt(miss_sq)
    pair_value = jnp.zeros((rows, LANES), F32)
    pair_slope = jnp.zeros((rows, LANES), F32)
    for i in range(1, members):
        pred_copies[i - 1].wait()
        delta = pred - preds_in[i].astype(F32)
        square = delta * delta + 0.0625
        inv = lax.rsqrt(square)
        pair_value = pair_value + square * inv
        pair_slope = pair_slope + delta * inv
    pair_scale = 1.0 / (members * (members - 1))
    share = weights * valid * (miss_sq * miss_inv / members - 0.5 * pair_scale * pair_value)
    part[...] = jnp.broadcast_to(jnp.sum(share, 0, keepdims=True), part.shape)
    loss_copies = [send(part, part_in.at[i], loss_sem, i, m, shard(i)) for i in range(1, shards)]
    for copy in loss_copies:
        copy.start()
    d_outb = (weights * (miss * miss_inv / members - pair_scale * pair_slope)).astype(BF)
    per_block = 256 // out_rows
    head_part = mm_tn(normed, d_outb) * scale
    for j in range(shards):
        ph[j] = head_part[j * out_rows : (j + 1) * out_rows].astype(BF)
    head_copies = [
        send(ph.at[shard(i)], ph_in.at[i], head_sem, i, m, shard(i)) for i in range(1, shards)
    ]
    for copy in head_copies:
        copy.start()
    d_normed = mm_nt(d_outb, wh[...])
    nhat = hidden[...]
    d_hid[...] = rstd * (
        d_normed
        - jnp.mean(d_normed, -1, keepdims=True)
        - nhat * jnp.mean(d_normed * nhat, -1, keepdims=True)
    )

    def dq_copy(c):
        slot = lax.rem(c - m + members, members)
        return send(dqs.at[c], dqs_in.at[slot], dq_sem, slot, c, s)

    def halo_copies(c):
        return [
            send(halo.at[0, c], halo_in.at[0, c], dth_sem, 2 * c, m, shard(shards - 1)),
            send(halo.at[1, c], halo_in.at[1, c], dth_sem, 2 * c + 1, m, shard(1)),
        ]

    for c in range(members):
        for t in range(per_chunk):
            p = c * per_chunk + t
            cols = slice(p * LANES, (p + 1) * LANES)
            here = slice(t * LANES, (t + 1) * LANES)
            there = slice(chunk + t * LANES, chunk + (t + 1) * LANES)
            d_out = d_hid[:, cols] * recip[:, cols]
            d_outl = d_out.astype(BF)
            kn = k_norm[:, cols]
            k2 = stacked(kn)
            v2 = stacked(table[:, width + p * LANES : width + (p + 1) * LANES].astype(F32))
            left = jnp.concatenate([d_outl, (d_out * mixed[:, cols]).astype(BF)], axis=1)
            d_weight = mm_nt(left, jnp.concatenate([v2, -in_head], axis=1))
            e = expo[p]
            d_score = (e.astype(F32) * d_weight * size ** (-0.5)).astype(BF)
            qn = q_norm[:, cols]
            d_qn = mm(d_score, k2)
            qf = qn.astype(F32)
            dqs[c, :, here] = (q_rstd[:, cols] * (d_qn - qf * head_mean(d_qn * qf))).astype(BF)
            d_kn = unstacked(mm_tn(d_score, qn))
            d_key = k_rstd[:, cols] * (d_kn - kn * head_mean(d_kn * kn))
            d_val = unstacked(mm_tn(e, d_outl))
            for where, grad in ((here, d_key), (there, d_val)):
                halo[0, c, :, where] = grad[:nodes].astype(BF)
                own_dt[c, :, where] = grad[nodes : 2 * nodes]
                halo[1, c, :, where] = grad[2 * nodes : 3 * nodes].astype(BF)
        for copy in halo_copies(c):
            copy.start()

        @pl.when(c != m)
        def _():
            dq_copy(c).start()

    total = part[...]
    for i in range(1, shards):
        loss_copies[i - 1].wait()
        total = total + part_in[i]
    loss_out[...] = jnp.broadcast_to(
        jnp.sum(total[0:1], -1, keepdims=True) / (rows * shards * variables), loss_out.shape
    )
    head_sum = ph[s].astype(F32)
    for i in range(1, shards):
        head_copies[i - 1].wait()
        head_sum = head_sum + ph_in[i].astype(F32)
    ph_fin[m] = head_sum.astype(BF)
    for i in range(1, members):
        pltpu.make_async_remote_copy(
            src_ref=ph_fin.at[m], dst_ref=ph_fin.at[m], send_sem=hfin_sem.at[0, i],
            recv_sem=hfin_sem.at[1, i], device_id=(member(i), s), device_id_type=MESH,
        ).start()

    for c in range(members):
        for copy in halo_copies(c):
            copy.wait()
        ob[c] = (own_dt[c] + halo_in[0, c].astype(F32) + halo_in[1, c].astype(F32)).astype(BF)

        @pl.when(c != m)
        def _():
            slot = lax.rem(c - m + members, members)
            send(ob.at[c], dt4.at[slot], dtm_sem, slot, c, s).start()

    dq_sum = dqs[m].astype(F32)
    for i in range(1, members):
        send(dqs.at[member(i)], dqs_in.at[i], dq_sem, i, member(i), s).wait()
        dq_sum = dq_sum + dqs_in[i].astype(F32)
    dq_sumb = dq_sum.astype(BF)
    for block in range(width // 256):
        piece = mm_tn(embed[:, block * 256 : (block + 1) * 256], dq_sumb) * scale
        for t in range(per_block):
            j = block * per_block + t
            pq[j % 2, j // 2] = piece[t * out_rows : (t + 1) * out_rows].astype(BF)
    partner = s + 1 - 2 * b
    y_query = send(pq.at[1 - b], yq, y_sem, 0, m, partner)
    y_query.start()

    dt4[0] = ob[m]
    for i in range(1, members):
        lat_copies[i - 1].wait()
        send(ob.at[member(i)], dt4.at[i], dtm_sem, i, member(i), s).wait()
    right = dt4[...].reshape(members * nodes, 2 * chunk)
    for block in range(width // 256):
        piece = mm_tn(lat4[:, block * 256 : (block + 1) * 256], right) * scale
        for t in range(per_block):
            j = block * per_block + t
            pk[j % 2, j // 2] = piece[t * out_rows : (t + 1) * out_rows].astype(BF)
    y_keyval = send(pk.at[1 - b], yk, y_sem, 1, m, partner)
    y_keyval.start()

    d_lat = jnp.zeros((nodes, width), F32)
    for c in range(members):
        d_lat = d_lat + mm_nt(ob[c, :, :chunk], w_keyval[:, c * chunk : (c + 1) * chunk])
        d_lat = d_lat + mm_nt(ob[c, :, chunk:], w_keyval[:, width + c * chunk : width + (c + 1) * chunk])
    d_latent[...] = d_lat

    def other(i):
        return lax.rem(a + i, outer)

    def z_copies(from_ref, in_ref, sems):
        return [
            send(from_ref.at[other(i)], in_ref.at[i], sems, i, m, 2 * other(i) + b)
            for i in range(1, outer)
        ]

    y_query.wait()
    zq[...] = (pq[b].astype(F32) + yq[...].astype(F32)).astype(BF)
    zq_copies = z_copies(zq, zq_in, zq_sem)
    for copy in zq_copies:
        copy.start()
    y_keyval.wait()
    zk[...] = (pk[b].astype(F32) + yk[...].astype(F32)).astype(BF)
    zk_copies = z_copies(zk, zk_in, zk_sem)
    for copy in zk_copies:
        copy.start()

    done = zq[a].astype(F32)
    for i in range(1, outer):
        zq_copies[i - 1].wait()
        done = done + zq_in[i].astype(F32)
    fq[...] = done.astype(BF)
    fq_copies = [send(fq, fq_in.at[i], fq_sem, i, member(i), s) for i in range(1, members)]
    for copy in fq_copies:
        copy.start()
    done = zk[a].astype(F32)
    for i in range(1, outer):
        zk_copies[i - 1].wait()
        done = done + zk_in[i].astype(F32)
    fk[...] = done.astype(BF)
    fk_copies = [send(fk, fk_in.at[i], fk_sem, i, member(i), s) for i in range(1, members)]
    for copy in fk_copies:
        copy.start()

    for i in range(1, members):
        pltpu.make_async_remote_copy(
            src_ref=ph_fin.at[m], dst_ref=ph_fin.at[member(members - i)], send_sem=hfin_sem.at[0, i],
            recv_sem=hfin_sem.at[1, i], device_id=(member(i), s), device_id_type=MESH,
        ).wait()
    head_total = ph_fin[0].astype(F32)
    for c in range(1, members):
        head_total = head_total + ph_fin[c].astype(F32)
    grad_head[...] = head_total[:, :variables]

    def at(start, i):
        return pl.ds(pl.multiple_of(start + member(members - i) * chunk, LANES), chunk)

    grad_query[:, at(0, 0)] = fq[...].astype(F32)
    for i in range(1, members):
        fq_copies[i - 1].wait()
        grad_query[:, at(0, i)] = fq_in[i].astype(F32)
    for i in range(members):
        if i:
            fk_copies[i - 1].wait()
        block = fk_in[i].astype(F32) if i else fk[...].astype(F32)
        grad_keyval[:, at(0, i)] = block[:, :chunk]
        grad_keyval[:, at(width, i)] = block[:, chunk:]


def on_device(latent, grid_embed, edge_src, area, target, w_query, w_keyval, w_head):
    rows, width = grid_embed.shape
    nodes = latent.shape[1]
    shards = lax.axis_size("shard")
    members = lax.axis_size("member")
    variables = target.shape[1]
    out_rows = width // shards
    chunk = width // members
    outer = shards // 2
    pairs = width // LANES
    padded = -(-3 * nodes // LANES) * LANES
    vm = pltpu.VMEM
    dma = lambda n: pltpu.SemaphoreType.DMA((2, n))
    outs = (
        jax.ShapeDtypeStruct((8, LANES), F32),
        jax.ShapeDtypeStruct((nodes, width), F32),
        jax.ShapeDtypeStruct((out_rows, width), F32),
        jax.ShapeDtypeStruct((out_rows, 2 * width), F32),
        jax.ShapeDtypeStruct((out_rows, variables), F32),
    )
    scratch = [
        vm((padded, width), BF),
        vm((members * nodes, width), BF),
        vm((padded, 2 * width), BF),
        vm((rows, width), F32),
        vm((rows, width), BF),
        vm((rows, width), F32),
        vm((padded, width), F32),
        vm((padded, width), F32),
        vm((pairs, rows, 2 * padded), BF),
        vm((rows, width), F32),
        vm((rows, width), F32),
        vm((rows, width), F32),
        vm((rows, width), F32),
        vm((width, LANES), BF),
        vm((rows, LANES), BF),
        vm((members, rows, LANES), BF),
        vm((shards, out_rows, LANES), BF),
        vm((shards, out_rows, LANES), BF),
        vm((members, out_rows, LANES), BF),
        vm((8, LANES), F32),
        vm((shards, 8, LANES), F32),
        vm((members, nodes, 2 * chunk), F32),
        vm((2, members, nodes, 2 * chunk), BF),
        vm((2, members, nodes, 2 * chunk), BF),
        vm((members, nodes, 2 * chunk), BF),
        vm((members, nodes, 2 * chunk), BF),
        vm((members, rows, chunk), BF),
        vm((members, rows, chunk), BF),
        vm((2, outer, out_rows, chunk), BF),
        vm((outer, out_rows, chunk), BF),
        vm((outer, out_rows, chunk), BF),
        vm((outer, out_rows, chunk), BF),
        vm((2, outer, out_rows, 2 * chunk), BF),
        vm((outer, out_rows, 2 * chunk), BF),
        vm((outer, out_rows, 2 * chunk), BF),
        vm((outer, out_rows, 2 * chunk), BF),
        vm((out_rows, chunk), BF),
        vm((out_rows, 2 * chunk), BF),
        vm((members, out_rows, chunk), BF),
        vm((members, out_rows, 2 * chunk), BF),
        dma(2), dma(members), dma(members), dma(shards), dma(shards), dma(members),
        dma(2 * members), dma(members), dma(members),
        dma(2), dma(outer), dma(outer), dma(members), dma(members),
    ]
    spec = pl.BlockSpec(memory_space=pltpu.VMEM)
    loss, d_lat, grad_q, grad_kv, grad_h = pl.pallas_call(
        functools.partial(kernel, members, shards),
        out_shape=outs,
        in_specs=[spec] * 8,
        out_specs=tuple([spec] * 5),
        scratch_shapes=scratch,
        compiler_params=pltpu.CompilerParams(
            collective_id=0, has_side_effects=True, vmem_limit_bytes=52 * 1024 * 1024
        ),
    )(latent[0], grid_embed, edge_src, area[:, None], target, w_query, w_keyval, w_head)
    return loss[0, :1], d_lat[None], grad_q, grad_kv, grad_h


def solution(mesh):
    placed = (
        P("member", "shard", None),
        P("shard", None),
        P("shard", None),
        P("shard"),
        P("shard", None),
        P(),
        P(),
        P(),
    )
    return jax.shard_map(
        on_device,
        mesh=mesh,
        in_specs=placed,
        out_specs=(
            P("member"),
            P("member", "shard", None),
            P("shard", None),
            P("shard", None),
            P("shard", None),
        ),
        check_vma=False,
    )
```

```python
import functools

import jax
import jax.numpy as jnp
from jax import lax
from jax.experimental import pallas as pl
from jax.experimental.pallas import tpu as pltpu
from jax.sharding import PartitionSpec as P

HEADS = 16
LANES = 128
BF = jnp.bfloat16
F32 = jnp.float32
MESH = pl.DeviceIdType.MESH


def mm(a, b):
    return jnp.dot(a, b, preferred_element_type=F32)


def mm_nt(a, b):
    return lax.dot_general(a, b, (((1,), (1,)), ((), ())), preferred_element_type=F32)


def mm_tn(a, b):
    return lax.dot_general(a, b, (((0,), (0,)), ((), ())), preferred_element_type=F32)


def kernel(
    members, shards,
    latent_hbm, embed_hbm, source, area, target, w_query_hbm, w_keyval_hbm, w_head,
    loss_out, d_latent, grad_query, grad_keyval, grad_head,
    latent, embed, w_query, w_keyval, meta,
    lat3, lat4, lat_t, lat_z, table, query, q_norm, q_rstd, k_norm, k_rstd, expo, recip, mixed, hidden, d_hid,
    wh, preds, preds_in, ph, ph_in, ph_fin, part, part_in,
    own_dt, halo, halo_in, ob, dt4, dqs, dqs_in, pq, yq, zq, zq_in, dtz, pk, yk, fq, fk,
    halo_sem, lat_sem, pred_sem, head_sem, loss_sem, hfin_sem, dth_sem, dtm_sem, dq_sem,
    y_sem, zq_sem, latz_sem, up_sem, down_sem, fq_sem, fk_sem, load_sem,
):
    loads = [
        pltpu.make_async_copy(src, dst, load_sem.at[i])
        for i, (src, dst) in enumerate(
            ((latent_hbm, latent), (embed_hbm, embed), (w_query_hbm, w_query), (w_keyval_hbm, w_keyval))
        )
    ]
    for load in loads:
        load.start()
    rows, width = embed.shape
    nodes = latent.shape[0]
    variables = target.shape[0]
    m = lax.axis_index("member")
    s = lax.axis_index("shard")
    size = width // HEADS
    pairs = width // LANES
    chunk = width // members
    per_chunk = chunk // LANES
    out_rows = width // shards
    outer = shards // 2
    a = s // 2
    b = lax.rem(s, 2)
    padded = lat3.shape[0]
    scale = (members * rows * shards) ** (-0.5)

    def send(src, dst, sems, index, to_m, to_s):
        return pltpu.make_async_remote_copy(
            src_ref=src, dst_ref=dst, send_sem=sems.at[0, index], recv_sem=sems.at[1, index],
            device_id=(to_m, to_s), device_id_type=MESH,
        )

    def member(i):
        return lax.rem(m + i, members)

    def shard(i):
        return lax.rem(s + i, shards)

    barrier = pltpu.get_barrier_semaphore()
    for i in range(1, members):
        pl.semaphore_signal(barrier, inc=1, device_id=(member(i), s), device_id_type=MESH)
    for i in range(1, shards):
        pl.semaphore_signal(barrier, inc=1, device_id=(m, shard(i)), device_id_type=MESH)
    pl.semaphore_wait(barrier, members + shards - 2)

    loads[0].wait()
    halo_up = send(latent, lat3.at[pl.ds(0, nodes)], halo_sem, 0, m, shard(1))
    halo_down = send(latent, lat3.at[pl.ds(2 * nodes, nodes)], halo_sem, 1, m, shard(shards - 1))
    halo_up.start()
    halo_down.start()
    lat_copies = [
        send(latent, lat4.at[pl.ds(i * nodes, nodes)], lat_sem, i, member(i), s) for i in range(1, members)
    ]
    for copy in lat_copies:
        copy.start()
    lat3[nodes : 2 * nodes, :] = latent[...]
    lat3[3 * nodes :, :] = jnp.zeros((padded - 3 * nodes, width), BF)
    lat4[:nodes, :] = latent[...]

    wh[...] = jnp.zeros(wh.shape, BF)
    wh[:variables, :] = w_head[...]
    meta[...] = jnp.zeros(meta.shape, F32)
    meta[:variables, :] = target[...]
    meta[104:105, :] = area[...]
    meta[112 : 112 + source.shape[0], :] = source[...].astype(F32)
    loads[1].wait()
    loads[2].wait()

    def query_step(i, carry):
        cols = pl.ds(pl.multiple_of(i * 256, 256), 256)
        query[:, cols] = mm(embed[...], w_query[:, cols])
        return carry

    lax.fori_loop(0, width // 256, query_step, 0)

    lane = lax.broadcasted_iota(jnp.int32, (1, LANES), 1)
    masks = [(lane // size == h).astype(F32) for h in range(2)]
    row_head = lax.broadcasted_iota(jnp.int32, (LANES, LANES), 0) // size
    col_head = lax.broadcasted_iota(jnp.int32, (LANES, LANES), 1) // size
    same = jnp.where(row_head == col_head, 1.0 / size, 0.0).astype(BF)

    def head_mean(x):
        return mm(x.astype(BF), same)

    def stacked(x):
        return jnp.concatenate([x * masks[0], x * masks[1]], axis=0).astype(BF)

    def unstacked(x):
        return x[:padded] * masks[0] + x[padded:] * masks[1]

    ones = jnp.ones((padded, LANES), F32)
    in_head = stacked(ones)
    turned = meta[...].T
    src = turned - ((s - 1) * nodes).astype(F32)
    src = jnp.where(src < 0, src + shards * nodes, src)
    src = jnp.where(src >= shards * nodes, src - shards * nodes, src)
    node = lax.broadcasted_iota(jnp.int32, (rows, padded), 1).astype(F32)
    count = jnp.zeros((rows, padded), F32)
    for k in range(source.shape[0]):
        count = count + (src[:, 112 + k : 113 + k] == node).astype(F32)
    count2 = jnp.concatenate([count, count], axis=1)

    halo_up.wait()
    halo_down.wait()
    loads[3].wait()

    def table_step(i, carry):
        cols = pl.ds(pl.multiple_of(i * 256, 256), 256)
        table[:, cols] = mm(lat3[...], w_keyval[:, cols]).astype(BF)
        return carry

    lax.fori_loop(0, 2 * width // 256, table_step, 0)

    for copy in lat_copies:
        copy.wait()
    held = members * nodes
    eye = lax.broadcasted_iota(jnp.int32, (held, held), 0) == lax.broadcasted_iota(jnp.int32, (held, held), 1)
    eye = eye.astype(F32).astype(BF)
    two = 2 * out_rows
    for block in range(width // 256):
        piece = mm_tn(lat4[:, block * 256 : (block + 1) * 256], eye).astype(BF)
        for t in range(256 // two):
            lat_t[block * (256 // two) + t] = piece[t * two : (t + 1) * two]

    def other(i):
        return lax.rem(a + i, outer)

    latz_copies = [
        send(lat_t.at[other(i)], lat_z.at[a], latz_sem, i, m, 2 * other(i) + b) for i in range(1, outer)
    ]
    for copy in latz_copies:
        copy.start()
    lat_z[a] = lat_t[a]

    for p in range(pairs):
        cols = slice(p * LANES, (p + 1) * LANES)
        q = query[:, cols]
        r = lax.rsqrt(head_mean(q * q) + 1e-06)
        qn = (q * r).astype(BF)
        q_norm[:, cols] = qn
        q_rstd[:, cols] = r
        key = table[:, cols].astype(F32)
        rk = lax.rsqrt(head_mean(key * key) + 1e-06)
        kn = key * rk
        k_norm[:, cols] = kn
        k_rstd[:, cols] = rk
        score = mm_nt(qn, stacked(kn))
        e = (count2 * jnp.exp(score * size ** (-0.5))).astype(BF)
        expo[p] = e
        v2 = stacked(table[:, width + p * LANES : width + (p + 1) * LANES].astype(F32))
        both = mm(e, jnp.concatenate([v2, in_head], axis=1))
        inv = 1.0 / both[:, LANES:]
        out = both[:, :LANES] * inv
        recip[:, cols] = inv
        mixed[:, cols] = out
        hidden[:, cols] = embed[:, cols].astype(F32) + out

    hid = hidden[...]
    center = hid - jnp.mean(hid, -1, keepdims=True)
    rstd = lax.rsqrt(jnp.mean(center * center, -1, keepdims=True) + 1e-05)
    nhat = center * rstd
    hidden[...] = nhat
    normed = nhat.astype(BF)
    pred = mm_nt(normed, wh[...])
    preds[...] = pred.astype(BF)
    pred_copies = [send(preds, preds_in.at[i], pred_sem, i, member(i), s) for i in range(1, members)]
    for copy in pred_copies:
        copy.start()
    valid = (lane < variables).astype(F32)
    weights = turned[:, 104:105]
    want = turned * valid
    miss = pred - want
    miss_sq = miss * miss + 0.0625
    miss_inv = lax.rsqrt(miss_sq)
    pair_value = jnp.zeros((rows, LANES), F32)
    pair_slope = jnp.zeros((rows, LANES), F32)
    for i in range(1, members):
        pred_copies[i - 1].wait()
        delta = pred - preds_in[i].astype(F32)
        square = delta * delta + 0.0625
        inv = lax.rsqrt(square)
        pair_value = pair_value + square * inv
        pair_slope = pair_slope + delta * inv
    pair_scale = 1.0 / (members * (members - 1))
    share = weights * valid * (miss_sq * miss_inv / members - 0.5 * pair_scale * pair_value)
    part[...] = jnp.broadcast_to(jnp.sum(share, 0, keepdims=True), part.shape)
    loss_copies = [send(part, part_in.at[i], loss_sem, i, m, shard(i)) for i in range(1, shards)]
    for copy in loss_copies:
        copy.start()
    d_outb = (weights * (miss * miss_inv / members - pair_scale * pair_slope)).astype(BF)
    per_block = 256 // out_rows
    head_part = mm_tn(normed, d_outb) * scale
    for j in range(shards):
        ph[j] = head_part[j * out_rows : (j + 1) * out_rows].astype(BF)
    head_copies = [
        send(ph.at[shard(i)], ph_in.at[i], head_sem, i, m, shard(i)) for i in range(1, shards)
    ]
    for copy in head_copies:
        copy.start()
    d_normed = mm(d_outb, wh[...])
    nhat = hidden[...]
    d_hid[...] = rstd * (
        d_normed
        - jnp.mean(d_normed, -1, keepdims=True)
        - nhat * jnp.mean(d_normed * nhat, -1, keepdims=True)
    )

    def dq_copy(c):
        slot = lax.rem(c - m + members, members)
        return send(dqs.at[c], dqs_in.at[slot], dq_sem, slot, c, s)

    def halo_copies(c):
        return [
            send(halo.at[0, c], halo_in.at[0, c], dth_sem, 2 * c, m, shard(shards - 1)),
            send(halo.at[1, c], halo_in.at[1, c], dth_sem, 2 * c + 1, m, shard(1)),
        ]

    for c in range(members):
        for t in range(per_chunk):
            p = c * per_chunk + t
            cols = slice(p * LANES, (p + 1) * LANES)
            here = slice(t * LANES, (t + 1) * LANES)
            there = slice(chunk + t * LANES, chunk + (t + 1) * LANES)
            d_out = d_hid[:, cols] * recip[:, cols]
            d_outl = d_out.astype(BF)
            kn = k_norm[:, cols]
            k2 = stacked(kn)
            v2 = stacked(table[:, width + p * LANES : width + (p + 1) * LANES].astype(F32))
            left = jnp.concatenate([d_outl, (d_out * mixed[:, cols]).astype(BF)], axis=1)
            d_weight = mm_nt(left, jnp.concatenate([v2, -in_head], axis=1))
            e = expo[p]
            d_score = (e.astype(F32) * d_weight * size ** (-0.5)).astype(BF)
            qn = q_norm[:, cols]
            d_qn = mm(d_score, k2)
            qf = qn.astype(F32)
            dqs[c, :, here] = (q_rstd[:, cols] * (d_qn - qf * head_mean(d_qn * qf))).astype(BF)
            d_kn = unstacked(mm_tn(d_score, qn))
            d_key = k_rstd[:, cols] * (d_kn - kn * head_mean(d_kn * kn))
            d_val = unstacked(mm_tn(e, d_outl))
            for where, grad in ((here, d_key), (there, d_val)):
                halo[0, c, :, where] = grad[:nodes].astype(BF)
                own_dt[c, :, where] = grad[nodes : 2 * nodes]
                halo[1, c, :, where] = grad[2 * nodes : 3 * nodes].astype(BF)
        for copy in halo_copies(c):
            copy.start()

        @pl.when(c != m)
        def _():
            dq_copy(c).start()

    total = part[...]
    for i in range(1, shards):
        loss_copies[i - 1].wait()
        total = total + part_in[i]
    loss_out[...] = jnp.sum(total[0:1], -1, keepdims=True) / (rows * shards * variables)
    head_sum = ph[s].astype(F32)
    for i in range(1, shards):
        head_copies[i - 1].wait()
        head_sum = head_sum + ph_in[i].astype(F32)
    ph_fin[m] = head_sum.astype(BF)
    for i in range(1, members):
        pltpu.make_async_remote_copy(
            src_ref=ph_fin.at[m], dst_ref=ph_fin.at[m], send_sem=hfin_sem.at[0, i],
            recv_sem=hfin_sem.at[1, i], device_id=(member(i), s), device_id_type=MESH,
        ).start()

    for c in range(members):
        for copy in halo_copies(c):
            copy.wait()
        ob[c] = (own_dt[c] + halo_in[0, c].astype(F32) + halo_in[1, c].astype(F32)).astype(BF)

        @pl.when(c != m)
        def _():
            slot = lax.rem(c - m + members, members)
            send(ob.at[c], dt4.at[slot], dtm_sem, slot, c, s).start()

    dq_sum = dqs[m].astype(F32)
    for i in range(1, members):
        send(dqs.at[member(i)], dqs_in.at[i], dq_sem, i, member(i), s).wait()
        dq_sum = dq_sum + dqs_in[i].astype(F32)
    dq_sumb = dq_sum.astype(BF)
    for block in range(width // 256):
        piece = mm_tn(embed[:, block * 256 : (block + 1) * 256], dq_sumb) * scale
        for t in range(per_block):
            j = block * per_block + t
            pq[j % 2, j // 2] = piece[t * out_rows : (t + 1) * out_rows].astype(BF)
    partner = s + 1 - 2 * b
    y_query = send(pq.at[1 - b], yq, y_sem, 0, m, partner)
    y_query.start()

    dt4[0] = ob[m]
    for i in range(1, members):
        send(ob.at[member(i)], dt4.at[i], dtm_sem, i, member(i), s).wait()
    dtz[a] = dt4[...].reshape(held, 2 * chunk)

    def upward(slot):
        return send(dtz.at[slot], dtz.at[slot], up_sem, slot, m, 2 * (a + 1) + b)

    def downward(slot):
        return send(dtz.at[slot], dtz.at[slot], down_sem, slot, m, 2 * (a - 1) + b)

    @pl.when(a < outer - 1)
    def _():
        upward(a).start()

    @pl.when(a > 0)
    def _():
        downward(a).start()

    d_lat = jnp.zeros((nodes, width), F32)
    for c in range(members):
        d_lat = d_lat + mm_nt(ob[c, :, :chunk], w_keyval[:, c * chunk : (c + 1) * chunk])
        d_lat = d_lat + mm_nt(ob[c, :, chunk:], w_keyval[:, width + c * chunk : width + (c + 1) * chunk])
    d_latent[...] = d_lat

    zq_copies = [
        send(zq.at[other(i)], zq_in.at[i], zq_sem, i, m, 2 * other(i) + b) for i in range(1, outer)
    ]
    for step in range(1, outer):

        @pl.when(a - step >= 0)
        def _():
            upward(a - step).wait_recv()

            @pl.when(a < outer - 1)
            def _():
                upward(a - step).start()

        @pl.when(a + step < outer)
        def _():
            downward(a + step).wait_recv()

            @pl.when(a > 0)
            def _():
                downward(a + step).start()

        if step == 1:
            y_query.wait()
            zq[...] = (pq[b].astype(F32) + yq[...].astype(F32)).astype(BF)
            for copy in zq_copies:
                copy.start()

    for copy in latz_copies:
        copy.wait()
    acc = jnp.zeros((two, 2 * chunk), F32)
    for t in range(outer):
        acc = acc + mm(lat_z[t], dtz[t])
    acc = acc * scale
    pk[0] = acc[:out_rows]
    pk[1] = acc[out_rows:]
    fk[m] = pk[1 - b].astype(BF)
    y_keyval = send(fk.at[m], yk, y_sem, 1, m, partner)
    y_keyval.start()

    core = lax.rem(m, 2)
    mate = m + 1 - 2 * core
    chips = members // 2

    def chip(i):
        return lax.rem(m + 2 * i, members)

    def spread(buffer, sems):
        out = [send(buffer.at[m], buffer.at[m], sems, i, chip(i), s) for i in range(1, chips)]
        out.append(send(buffer.at[m], buffer.at[m], sems, chips, mate, s))
        for copy in out:
            copy.start()
        return out

    def forward(buffer, sems, i):
        slot = chip(chips - i)
        return send(buffer.at[slot], buffer.at[slot], sems, chips + i, mate, s)

    done = zq[a].astype(F32)
    for i in range(1, outer):
        zq_copies[i - 1].wait()
        done = done + zq_in[i].astype(F32)
    fq[m] = done.astype(BF)
    q_copies = spread(fq, fq_sem)
    y_keyval.wait()
    fk[m] = (pk[b] + yk[...].astype(F32)).astype(BF)
    k_copies = spread(fk, fk_sem)

    for i in range(1, members):
        pltpu.make_async_remote_copy(
            src_ref=ph_fin.at[m], dst_ref=ph_fin.at[member(members - i)], send_sem=hfin_sem.at[0, i],
            recv_sem=hfin_sem.at[1, i], device_id=(member(i), s), device_id_type=MESH,
        ).wait()
    head_total = ph_fin[0].astype(F32)
    for c in range(1, members):
        head_total = head_total + ph_fin[c].astype(F32)
    grad_head[...] = head_total.T[:variables]

    for buffer, sems, copies in ((fq, fq_sem, q_copies), (fk, fk_sem, k_copies)):
        for i in range(1, chips):
            copies[i - 1].wait()
            forward(buffer, sems, i).start()
    for buffer, sems, copies in ((fq, fq_sem, q_copies), (fk, fk_sem, k_copies)):
        copies[-1].wait()
        for i in range(1, chips):
            forward(buffer, sems, i).wait()
    for c in range(members):
        grad_query[:, c * chunk : (c + 1) * chunk] = fq[c]
        grad_keyval[:, c * chunk : (c + 1) * chunk] = fk[c, :, :chunk]
        grad_keyval[:, width + c * chunk : width + (c + 1) * chunk] = fk[c, :, chunk:]

    for slot in range(outer):

        @pl.when((a < outer - 1) & (a >= slot))
        def _():
            upward(slot).wait_send()

        @pl.when((a > 0) & (a <= slot))
        def _():
            downward(slot).wait_send()


def on_device(latent, grid_embed, edge_src, area, target, w_query, w_keyval, w_head):
    rows, width = grid_embed.shape
    nodes = latent.shape[1]
    shards = lax.axis_size("shard")
    members = lax.axis_size("member")
    variables = target.shape[1]
    held = members * nodes
    out_rows = width // shards
    chunk = width // members
    outer = shards // 2
    pairs = width // LANES
    padded = -(-3 * nodes // LANES) * LANES
    vm = pltpu.VMEM
    dma = lambda n: pltpu.SemaphoreType.DMA((2, n))
    outs = (
        jax.ShapeDtypeStruct((1, 1), F32),
        jax.ShapeDtypeStruct((nodes, width), F32),
        jax.ShapeDtypeStruct((out_rows, width), BF),
        jax.ShapeDtypeStruct((out_rows, 2 * width), BF),
        jax.ShapeDtypeStruct((variables, out_rows), F32),
    )
    scratch = [
        vm((nodes, width), BF),
        vm((rows, width), BF),
        vm((width, width), BF),
        vm((width, 2 * width), BF),
        vm((LANES, rows), F32),
        vm((padded, width), BF),
        vm((held, width), BF),
        vm((outer, 2 * out_rows, held), BF),
        vm((outer, 2 * out_rows, held), BF),
        vm((padded, 2 * width), BF),
        vm((rows, width), F32),
        vm((rows, width), BF),
        vm((rows, width), F32),
        vm((padded, width), F32),
        vm((padded, width), F32),
        vm((pairs, rows, 2 * padded), BF),
        vm((rows, width), F32),
        vm((rows, width), F32),
        vm((rows, width), F32),
        vm((rows, width), F32),
        vm((LANES, width), BF),
        vm((rows, LANES), BF),
        vm((members, rows, LANES), BF),
        vm((shards, out_rows, LANES), BF),
        vm((shards, out_rows, LANES), BF),
        vm((members, out_rows, LANES), BF),
        vm((8, LANES), F32),
        vm((shards, 8, LANES), F32),
        vm((members, nodes, 2 * chunk), F32),
        vm((2, members, nodes, 2 * chunk), BF),
        vm((2, members, nodes, 2 * chunk), BF),
        vm((members, nodes, 2 * chunk), BF),
        vm((members, nodes, 2 * chunk), BF),
        vm((members, rows, chunk), BF),
        vm((members, rows, chunk), BF),
        vm((2, outer, out_rows, chunk), BF),
        vm((outer, out_rows, chunk), BF),
        vm((outer, out_rows, chunk), BF),
        vm((outer, out_rows, chunk), BF),
        vm((outer, held, 2 * chunk), BF),
        vm((2, out_rows, 2 * chunk), F32),
        vm((out_rows, 2 * chunk), BF),
        vm((members, out_rows, chunk), BF),
        vm((members, out_rows, 2 * chunk), BF),
        dma(2), dma(members), dma(members), dma(shards), dma(shards), dma(members),
        dma(2 * members), dma(members), dma(members),
        dma(2), dma(outer), dma(outer), dma(outer), dma(outer), dma(members), dma(members),
        pltpu.SemaphoreType.DMA((4,)),
    ]
    spec = pl.BlockSpec(memory_space=pltpu.VMEM)
    hbm = pl.BlockSpec(memory_space=pl.ANY)
    loss, d_lat, grad_q, grad_kv, grad_h = pl.pallas_call(
        functools.partial(kernel, members, shards),
        out_shape=outs,
        in_specs=[hbm, hbm, spec, spec, spec, hbm, hbm, spec],
        out_specs=tuple([spec] * 5),
        scratch_shapes=scratch,
        compiler_params=pltpu.CompilerParams(
            collective_id=0, has_side_effects=True, vmem_limit_bytes=52 * 1024 * 1024
        ),
    )(latent[0], grid_embed, edge_src.T, area[None], target.T, w_query, w_keyval, w_head.T)
    return loss[0], d_lat[None], grad_q.astype(F32), grad_kv.astype(F32), grad_h.T


def solution(mesh):
    placed = (
        P("member", "shard", None),
        P("shard", None),
        P("shard", None),
        P("shard"),
        P("shard", None),
        P(),
        P(),
        P(),
    )
    return jax.shard_map(
        on_device,
        mesh=mesh,
        in_specs=placed,
        out_specs=(
            P("member"),
            P("member", "shard", None),
            P("shard", None),
            P("shard", None),
            P("shard", None),
        ),
        check_vma=False,
    )
```

```python
import functools

import jax
import jax.numpy as jnp
from jax import lax
from jax.experimental import pallas as pl
from jax.experimental.pallas import tpu as pltpu
from jax.sharding import PartitionSpec as P

HEADS = 16
LANES = 128
BF = jnp.bfloat16
F32 = jnp.float32
MESH = pl.DeviceIdType.MESH


def mm(a, b):
    return jnp.dot(a, b, preferred_element_type=F32)


def mm_nt(a, b):
    return lax.dot_general(a, b, (((1,), (1,)), ((), ())), preferred_element_type=F32)


def mm_tn(a, b):
    return lax.dot_general(a, b, (((0,), (0,)), ((), ())), preferred_element_type=F32)


def kernel(
    members, shards,
    latent_hbm, embed_hbm, source_hbm, area_hbm, target_hbm, w_query_hbm, w_keyval_hbm, w_head_hbm,
    loss_out, d_latent, grad_query, grad_keyval, grad_head,
    latent, embed, source, area, target, w_query, w_keyval, w_head, meta,
    lat3, lat4, lat_t, lat_z, table, query, q_norm, q_rstd, k_norm, k_rstd, expo, recip, mixed, hidden, d_hid,
    wh, preds, preds_in, ph, ph_in, ph_fin, part, part_in,
    own_dt, halo, halo_in, ob, dt4, dqs, dqs_in, pq, yq, zq, zq_in, dtz, pk, yk, fq, fk,
    halo_sem, lat_sem, pred_sem, head_sem, loss_sem, hfin_sem, dth_sem, dtm_sem, dq_sem,
    y_sem, zq_sem, latz_sem, up_sem, down_sem, fq_sem, fk_sem, load_sem,
):
    loads = [
        pltpu.make_async_copy(src, dst, load_sem.at[i])
        for i, (src, dst) in enumerate(
            (
                (latent_hbm, latent), (embed_hbm, embed), (w_query_hbm, w_query), (source_hbm, source),
                (area_hbm, area), (target_hbm, target), (w_head_hbm, w_head), (w_keyval_hbm, w_keyval),
            )
        )
    ]
    for load in loads:
        load.start()
    rows, width = embed.shape
    nodes = latent.shape[0]
    variables = target.shape[0]
    m = lax.axis_index("member")
    s = lax.axis_index("shard")
    size = width // HEADS
    pairs = width // LANES
    chunk = width // members
    per_chunk = chunk // LANES
    out_rows = width // shards
    outer = shards // 2
    a = s // 2
    b = lax.rem(s, 2)
    padded = lat3.shape[0]
    scale = (members * rows * shards) ** (-0.5)

    def send(src, dst, sems, index, to_m, to_s):
        return pltpu.make_async_remote_copy(
            src_ref=src, dst_ref=dst, send_sem=sems.at[0, index], recv_sem=sems.at[1, index],
            device_id=(to_m, to_s), device_id_type=MESH,
        )

    def member(i):
        return lax.rem(m + i, members)

    def shard(i):
        return lax.rem(s + i, shards)

    barrier = pltpu.get_barrier_semaphore()
    for i in range(1, members):
        pl.semaphore_signal(barrier, inc=1, device_id=(member(i), s), device_id_type=MESH)
    for i in range(1, shards):
        pl.semaphore_signal(barrier, inc=1, device_id=(m, shard(i)), device_id_type=MESH)
    pl.semaphore_wait(barrier, members + shards - 2)

    loads[0].wait()
    halo_up = send(latent, lat3.at[pl.ds(0, nodes)], halo_sem, 0, m, shard(1))
    halo_down = send(latent, lat3.at[pl.ds(2 * nodes, nodes)], halo_sem, 1, m, shard(shards - 1))
    halo_up.start()
    halo_down.start()
    lat_copies = [
        send(latent, lat4.at[pl.ds(i * nodes, nodes)], lat_sem, i, member(i), s) for i in range(1, members)
    ]
    for copy in lat_copies:
        copy.start()
    lat3[nodes : 2 * nodes, :] = latent[...]
    lat3[3 * nodes :, :] = jnp.zeros((padded - 3 * nodes, width), BF)
    lat4[:nodes, :] = latent[...]

    for load in loads[1:7]:
        load.wait()
    wh[...] = jnp.zeros(wh.shape, BF)
    wh[:variables, :] = w_head[...]
    meta[...] = jnp.zeros(meta.shape, F32)
    meta[:variables, :] = target[...]
    meta[104:105, :] = area[...]
    meta[112 : 112 + source.shape[0], :] = source[...].astype(F32)


    def query_step(i, carry):
        cols = pl.ds(pl.multiple_of(i * 256, 256), 256)
        query[:, cols] = mm(embed[...], w_query[:, cols])
        return carry

    lax.fori_loop(0, width // 256, query_step, 0)

    lane = lax.broadcasted_iota(jnp.int32, (1, LANES), 1)
    masks = [(lane // size == h).astype(F32) for h in range(2)]
    row_head = lax.broadcasted_iota(jnp.int32, (LANES, LANES), 0) // size
    col_head = lax.broadcasted_iota(jnp.int32, (LANES, LANES), 1) // size
    same = jnp.where(row_head == col_head, 1.0 / size, 0.0).astype(BF)

    def head_mean(x):
        return mm(x.astype(BF), same)

    def stacked(x):
        return jnp.concatenate([x * masks[0], x * masks[1]], axis=0).astype(BF)

    def unstacked(x):
        return x[:padded] * masks[0] + x[padded:] * masks[1]

    ones = jnp.ones((padded, LANES), F32)
    in_head = stacked(ones)
    turned = meta[...].T
    src = turned - ((s - 1) * nodes).astype(F32)
    src = jnp.where(src < 0, src + shards * nodes, src)
    src = jnp.where(src >= shards * nodes, src - shards * nodes, src)
    node = lax.broadcasted_iota(jnp.int32, (rows, padded), 1).astype(F32)
    count = jnp.zeros((rows, padded), F32)
    for k in range(source.shape[0]):
        count = count + (src[:, 112 + k : 113 + k] == node).astype(F32)
    count2 = jnp.concatenate([count, count], axis=1)

    halo_up.wait()
    halo_down.wait()
    loads[7].wait()

    def table_step(i, carry):
        cols = pl.ds(pl.multiple_of(i * 256, 256), 256)
        table[:, cols] = mm(lat3[...], w_keyval[:, cols]).astype(BF)
        return carry

    lax.fori_loop(0, 2 * width // 256, table_step, 0)

    for copy in lat_copies:
        copy.wait()
    held = members * nodes
    eye = lax.broadcasted_iota(jnp.int32, (held, held), 0) == lax.broadcasted_iota(jnp.int32, (held, held), 1)
    eye = eye.astype(F32).astype(BF)
    two = 2 * out_rows
    for block in range(width // 256):
        piece = mm_tn(lat4[:, block * 256 : (block + 1) * 256], eye).astype(BF)
        for t in range(256 // two):
            lat_t[block * (256 // two) + t] = piece[t * two : (t + 1) * two]

    def other(i):
        return lax.rem(a + i, outer)

    latz_copies = [
        send(lat_t.at[other(i)], lat_z.at[a], latz_sem, i, m, 2 * other(i) + b) for i in range(1, outer)
    ]
    for copy in latz_copies:
        copy.start()
    lat_z[a] = lat_t[a]

    for p in range(pairs):
        cols = slice(p * LANES, (p + 1) * LANES)
        q = query[:, cols]
        r = lax.rsqrt(head_mean(q * q) + 1e-06)
        qn = (q * r).astype(BF)
        q_norm[:, cols] = qn
        q_rstd[:, cols] = r
        key = table[:, cols].astype(F32)
        rk = lax.rsqrt(head_mean(key * key) + 1e-06)
        kn = key * rk
        k_norm[:, cols] = kn
        k_rstd[:, cols] = rk
        score = mm_nt(qn, stacked(kn))
        e = (count2 * jnp.exp(score * size ** (-0.5))).astype(BF)
        expo[p] = e
        v2 = stacked(table[:, width + p * LANES : width + (p + 1) * LANES].astype(F32))
        both = mm(e, jnp.concatenate([v2, in_head], axis=1))
        inv = 1.0 / both[:, LANES:]
        out = both[:, :LANES] * inv
        recip[:, cols] = inv
        mixed[:, cols] = out
        hidden[:, cols] = embed[:, cols].astype(F32) + out

    hid = hidden[...]
    center = hid - jnp.mean(hid, -1, keepdims=True)
    rstd = lax.rsqrt(jnp.mean(center * center, -1, keepdims=True) + 1e-05)
    nhat = center * rstd
    hidden[...] = nhat
    normed = nhat.astype(BF)
    pred = mm_nt(normed, wh[...])
    preds[...] = pred.astype(BF)
    pred_copies = [send(preds, preds_in.at[i], pred_sem, i, member(i), s) for i in range(1, members)]
    for copy in pred_copies:
        copy.start()
    valid = (lane < variables).astype(F32)
    weights = turned[:, 104:105]
    want = turned * valid
    miss = pred - want
    miss_sq = miss * miss + 0.0625
    miss_inv = lax.rsqrt(miss_sq)
    pair_value = jnp.zeros((rows, LANES), F32)
    pair_slope = jnp.zeros((rows, LANES), F32)
    for i in range(1, members):
        pred_copies[i - 1].wait()
        delta = pred - preds_in[i].astype(F32)
        square = delta * delta + 0.0625
        inv = lax.rsqrt(square)
        pair_value = pair_value + square * inv
        pair_slope = pair_slope + delta * inv
    pair_scale = 1.0 / (members * (members - 1))
    share = weights * valid * (miss_sq * miss_inv / members - 0.5 * pair_scale * pair_value)
    part[...] = jnp.broadcast_to(jnp.sum(share, 0, keepdims=True), part.shape)
    loss_copies = [send(part, part_in.at[i], loss_sem, i, m, shard(i)) for i in range(1, shards)]
    for copy in loss_copies:
        copy.start()
    d_outb = (weights * (miss * miss_inv / members - pair_scale * pair_slope)).astype(BF)
    per_block = 256 // out_rows
    head_part = mm_tn(normed, d_outb) * scale
    for j in range(shards):
        ph[j] = head_part[j * out_rows : (j + 1) * out_rows].astype(BF)
    head_copies = [
        send(ph.at[shard(i)], ph_in.at[i], head_sem, i, m, shard(i)) for i in range(1, shards)
    ]
    for copy in head_copies:
        copy.start()
    d_normed = mm(d_outb, wh[...])
    nhat = hidden[...]
    d_hid[...] = rstd * (
        d_normed
        - jnp.mean(d_normed, -1, keepdims=True)
        - nhat * jnp.mean(d_normed * nhat, -1, keepdims=True)
    )

    def dq_copies(t):
        return [
            send(dqs.at[t, member(i)], dqs_in.at[t, i], dq_sem, t * members + i, member(i), s)
            for i in range(1, members)
        ]

    def halo_copies(t):
        return [
            send(halo.at[0, t], halo_in.at[0, t], dth_sem, 2 * t, m, shard(shards - 1)),
            send(halo.at[1, t], halo_in.at[1, t], dth_sem, 2 * t + 1, m, shard(1)),
        ]

    def dtm_copies(t):
        return [
            send(ob.at[t, member(i)], dt4.at[t, i], dtm_sem, t * members + i, member(i), s)
            for i in range(1, members)
        ]

    def own_block(t):
        for copy in halo_copies(t):
            copy.wait()
        ob[t] = (own_dt[t] + halo_in[0, t].astype(F32) + halo_in[1, t].astype(F32)).astype(BF)
        for copy in dtm_copies(t):
            copy.start()

    def upward(t, slot):
        return send(dtz.at[t, slot], dtz.at[t, slot], up_sem, t * outer + slot, m, 2 * (a + 1) + b)

    def downward(t, slot):
        return send(dtz.at[t, slot], dtz.at[t, slot], down_sem, t * outer + slot, m, 2 * (a - 1) + b)

    def line_start(t):
        dt4[t, 0] = ob[t, m]
        for copy in dtm_copies(t):
            copy.wait()
        dtz[t, a] = dt4[t].reshape(held, 2 * LANES)

        @pl.when(a < outer - 1)
        def _():
            upward(t, a).start()

        @pl.when(a > 0)
        def _():
            downward(t, a).start()

    def line_step(t, step):
        @pl.when(a - step >= 0)
        def _():
            upward(t, a - step).wait_recv()

            @pl.when(a < outer - 1)
            def _():
                upward(t, a - step).start()

        @pl.when(a + step < outer)
        def _():
            downward(t, a + step).wait_recv()

            @pl.when(a > 0)
            def _():
                downward(t, a + step).start()

    for t in range(per_chunk):
        for c in range(members):
            p = t * members + c
            if t > 0 and c == members // 2:
                own_block(t - 1)
            here = slice(0, LANES)
            there = slice(LANES, 2 * LANES)
            cols = slice(p * LANES, (p + 1) * LANES)
            d_out = d_hid[:, cols] * recip[:, cols]
            d_outl = d_out.astype(BF)
            kn = k_norm[:, cols]
            k2 = stacked(kn)
            v2 = stacked(table[:, width + p * LANES : width + (p + 1) * LANES].astype(F32))
            left = jnp.concatenate([d_outl, (d_out * mixed[:, cols]).astype(BF)], axis=1)
            d_weight = mm_nt(left, jnp.concatenate([v2, -in_head], axis=1))
            e = expo[p]
            d_score = (e.astype(F32) * d_weight * size ** (-0.5)).astype(BF)
            qn = q_norm[:, cols]
            d_qn = mm(d_score, k2)
            qf = qn.astype(F32)
            dqs[t, c] = (q_rstd[:, cols] * (d_qn - qf * head_mean(d_qn * qf))).astype(BF)
            d_kn = unstacked(mm_tn(d_score, qn))
            d_key = k_rstd[:, cols] * (d_kn - kn * head_mean(d_kn * kn))
            d_val = unstacked(mm_tn(e, d_outl))
            for where, grad in ((here, d_key), (there, d_val)):
                halo[0, t, c, :, where] = grad[:nodes].astype(BF)
                own_dt[t, c, :, where] = grad[nodes : 2 * nodes]
                halo[1, t, c, :, where] = grad[2 * nodes : 3 * nodes].astype(BF)
        for copy in halo_copies(t) + dq_copies(t):
            copy.start()
        if t > 0:
            line_start(t - 1)

    total = part[...]
    for i in range(1, shards):
        loss_copies[i - 1].wait()
        total = total + part_in[i]
    loss_out[...] = jnp.sum(total[0:1], -1, keepdims=True) / (rows * shards * variables)
    head_sum = ph[s].astype(F32)
    for i in range(1, shards):
        head_copies[i - 1].wait()
        head_sum = head_sum + ph_in[i].astype(F32)
    ph_fin[m] = head_sum.astype(BF)
    for i in range(1, members):
        pltpu.make_async_remote_copy(
            src_ref=ph_fin.at[m], dst_ref=ph_fin.at[m], send_sem=hfin_sem.at[0, i],
            recv_sem=hfin_sem.at[1, i], device_id=(member(i), s), device_id_type=MESH,
        ).start()

    last = per_chunk - 1
    own_block(last)
    dq_sums = []
    for t in range(per_chunk):
        dq_sum = dqs[t, m].astype(F32)
        for i, copy in enumerate(dq_copies(t)):
            copy.wait()
            dq_sum = dq_sum + dqs_in[t, i + 1].astype(F32)
        dq_sums.append(dq_sum)
    dq_sum = jnp.concatenate(dq_sums, axis=1) if per_chunk > 1 else dq_sums[0]
    dq_sumb = dq_sum.astype(BF)
    for block in range(width // 256):
        piece = mm_tn(embed[:, block * 256 : (block + 1) * 256], dq_sumb) * scale
        for t in range(per_block):
            j = block * per_block + t
            pq[j % 2, j // 2] = piece[t * out_rows : (t + 1) * out_rows].astype(BF)
    partner = s + 1 - 2 * b
    y_query = send(pq.at[1 - b], yq, y_sem, 0, m, partner)
    y_query.start()

    line_start(last)

    d_lat = jnp.zeros((nodes, width), F32)
    for p in range(pairs):
        block = ob[p // members, p % members]
        d_lat = d_lat + mm_nt(block[:, :LANES], w_keyval[:, p * LANES : (p + 1) * LANES])
        d_lat = d_lat + mm_nt(
            block[:, LANES:], w_keyval[:, width + p * LANES : width + (p + 1) * LANES]
        )
    d_latent[...] = d_lat

    zq_copies = [
        send(zq.at[other(i)], zq_in.at[i], zq_sem, i, m, 2 * other(i) + b) for i in range(1, outer)
    ]
    for step in range(1, outer):
        for t in range(per_chunk):
            line_step(t, step)
        if step == 1:
            y_query.wait()
            zq[...] = (pq[b].astype(F32) + yq[...].astype(F32)).astype(BF)
            for copy in zq_copies:
                copy.start()

    for copy in latz_copies:
        copy.wait()
    accs = []
    for t in range(per_chunk):
        acc = jnp.zeros((two, 2 * LANES), F32)
        for x in range(outer):
            acc = acc + mm(lat_z[x], dtz[t, x])
        accs.append(acc)
    acc = jnp.concatenate(accs, axis=1) if per_chunk > 1 else accs[0]
    acc = acc * scale
    pk[0] = acc[:out_rows]
    pk[1] = acc[out_rows:]
    fk[m] = pk[1 - b].astype(BF)
    y_keyval = send(fk.at[m], yk, y_sem, 1, m, partner)
    y_keyval.start()

    core = lax.rem(m, 2)
    mate = m + 1 - 2 * core
    chips = members // 2

    def chip(i):
        return lax.rem(m + 2 * i, members)

    def spread(buffer, sems):
        out = [send(buffer.at[m], buffer.at[m], sems, i, chip(i), s) for i in range(1, chips)]
        out.append(send(buffer.at[m], buffer.at[m], sems, chips, mate, s))
        for copy in out:
            copy.start()
        return out

    def forward(buffer, sems, i):
        slot = chip(chips - i)
        return send(buffer.at[slot], buffer.at[slot], sems, chips + i, mate, s)

    done = zq[a].astype(F32)
    for i in range(1, outer):
        zq_copies[i - 1].wait()
        done = done + zq_in[i].astype(F32)
    fq[m] = done.astype(BF)
    q_copies = spread(fq, fq_sem)
    y_keyval.wait()
    fk[m] = (pk[b] + yk[...].astype(F32)).astype(BF)
    k_copies = spread(fk, fk_sem)

    for i in range(1, members):
        pltpu.make_async_remote_copy(
            src_ref=ph_fin.at[m], dst_ref=ph_fin.at[member(members - i)], send_sem=hfin_sem.at[0, i],
            recv_sem=hfin_sem.at[1, i], device_id=(member(i), s), device_id_type=MESH,
        ).wait()
    head_total = ph_fin[0].astype(F32)
    for c in range(1, members):
        head_total = head_total + ph_fin[c].astype(F32)
    grad_head[...] = head_total.T[:variables]

    for buffer, sems, copies in ((fq, fq_sem, q_copies), (fk, fk_sem, k_copies)):
        for i in range(1, chips):
            copies[i - 1].wait()
            forward(buffer, sems, i).start()
    for buffer, sems, copies in ((fq, fq_sem, q_copies), (fk, fk_sem, k_copies)):
        copies[-1].wait()
        for i in range(1, chips):
            forward(buffer, sems, i).wait()
    for p in range(pairs):
        t, c = p // members, p % members
        cols = slice(p * LANES, (p + 1) * LANES)
        grad_query[:, cols] = fq[c, :, t * LANES : (t + 1) * LANES]
        grad_keyval[:, cols] = fk[c, :, 2 * t * LANES : (2 * t + 1) * LANES]
        grad_keyval[:, width + p * LANES : width + (p + 1) * LANES] = fk[
            c, :, (2 * t + 1) * LANES : (2 * t + 2) * LANES
        ]

    for t in range(per_chunk):
        for slot in range(outer):

            @pl.when((a < outer - 1) & (a >= slot))
            def _():
                upward(t, slot).wait_send()

            @pl.when((a > 0) & (a <= slot))
            def _():
                downward(t, slot).wait_send()


def on_device(latent, grid_embed, edge_src, area, target, w_query, w_keyval, w_head):
    rows, width = grid_embed.shape
    nodes = latent.shape[1]
    shards = lax.axis_size("shard")
    members = lax.axis_size("member")
    variables = target.shape[1]
    held = members * nodes
    out_rows = width // shards
    chunk = width // members
    outer = shards // 2
    pairs = width // LANES
    groups = chunk // LANES
    padded = -(-3 * nodes // LANES) * LANES
    vm = pltpu.VMEM
    dma = lambda n: pltpu.SemaphoreType.DMA((2, n))
    outs = (
        jax.ShapeDtypeStruct((1, 1), F32),
        jax.ShapeDtypeStruct((nodes, width), F32),
        jax.ShapeDtypeStruct((out_rows, width), BF),
        jax.ShapeDtypeStruct((out_rows, 2 * width), BF),
        jax.ShapeDtypeStruct((variables, out_rows), F32),
    )
    scratch = [
        vm((nodes, width), BF),
        vm((rows, width), BF),
        vm((edge_src.shape[1], rows), jnp.int32),
        vm((1, rows), F32),
        vm((variables, rows), F32),
        vm((width, width), BF),
        vm((width, 2 * width), BF),
        vm((variables, width), BF),
        vm((LANES, rows), F32),
        vm((padded, width), BF),
        vm((held, width), BF),
        vm((outer, 2 * out_rows, held), BF),
        vm((outer, 2 * out_rows, held), BF),
        vm((padded, 2 * width), BF),
        vm((rows, width), F32),
        vm((rows, width), BF),
        vm((rows, width), F32),
        vm((padded, width), F32),
        vm((padded, width), F32),
        vm((pairs, rows, 2 * padded), BF),
        vm((rows, width), F32),
        vm((rows, width), F32),
        vm((rows, width), F32),
        vm((rows, width), F32),
        vm((LANES, width), BF),
        vm((rows, LANES), BF),
        vm((members, rows, LANES), BF),
        vm((shards, out_rows, LANES), BF),
        vm((shards, out_rows, LANES), BF),
        vm((members, out_rows, LANES), BF),
        vm((8, LANES), F32),
        vm((shards, 8, LANES), F32),
        vm((groups, members, nodes, 2 * LANES), F32),
        vm((2, groups, members, nodes, 2 * LANES), BF),
        vm((2, groups, members, nodes, 2 * LANES), BF),
        vm((groups, members, nodes, 2 * LANES), BF),
        vm((groups, members, nodes, 2 * LANES), BF),
        vm((groups, members, rows, LANES), BF),
        vm((groups, members, rows, LANES), BF),
        vm((2, outer, out_rows, chunk), BF),
        vm((outer, out_rows, chunk), BF),
        vm((outer, out_rows, chunk), BF),
        vm((outer, out_rows, chunk), BF),
        vm((groups, outer, held, 2 * LANES), BF),
        vm((2, out_rows, 2 * chunk), F32),
        vm((out_rows, 2 * chunk), BF),
        vm((members, out_rows, chunk), BF),
        vm((members, out_rows, 2 * chunk), BF),
        dma(2), dma(members), dma(members), dma(shards), dma(shards), dma(members),
        dma(2 * groups), dma(groups * members), dma(groups * members),
        dma(2), dma(outer), dma(outer), dma(groups * outer), dma(groups * outer), dma(members), dma(members),
        pltpu.SemaphoreType.DMA((8,)),
    ]
    spec = pl.BlockSpec(memory_space=pltpu.VMEM)
    hbm = pl.BlockSpec(memory_space=pltpu.HBM)
    loss, d_lat, grad_q, grad_kv, grad_h = pl.pallas_call(
        functools.partial(kernel, members, shards),
        out_shape=outs,
        in_specs=[hbm] * 8,
        out_specs=tuple([spec] * 5),
        scratch_shapes=scratch,
        compiler_params=pltpu.CompilerParams(
            collective_id=0, has_side_effects=True, vmem_limit_bytes=63 * 1024 * 1024
        ),
    )(latent[0], grid_embed, edge_src.T, area[None], target.T, w_query, w_keyval, w_head.T)
    return loss[0], d_lat[None], grad_q.astype(F32), grad_kv.astype(F32), grad_h.T


def solution(mesh):
    placed = (
        P("member", "shard", None),
        P("shard", None),
        P("shard", None),
        P("shard"),
        P("shard", None),
        P(),
        P(),
        P(),
    )
    return jax.shard_map(
        on_device,
        mesh=mesh,
        in_specs=placed,
        out_specs=(
            P("member"),
            P("member", "shard", None),
            P("shard", None),
            P("shard", None),
            P("shard", None),
        ),
        check_vma=False,
    )
```
